32 devices in a mesh: axial: 16 (over z, y, core), circ: 2 (over x).
Axes of the slice: x: 2, y: 2, z: 4, core: 2. Of those that a mesh axis runs over, the one named last changes fastest.
Arguments:
- mode_shapes: float32 [32, 4, 128, 512], P('axial', 'circ'), may hold values from -0.0625 to 0.0625
- amplitude: float32 [32, 4, 128], P('axial', 'circ'), may hold values from 0.3 to 3
- pair_list: int32 [16, 2, 3, 20], P('axial', 'circ'), may hold values from -1 to 3, as said below
- pair_counts: int32 [16, 2], P('axial', 'circ'), may hold values from 2 to 20, as said below
Outputs:
- modal_spectrum: float32 [2, 512, 512], P(None, 'axial', 'circ')
The draws below stay inside these ranges and needn't reach their ends.
Inputs may be any that keep to these rules, and one draw needn't show every extreme that they name: `pair_list`: each device's 20 slots hold distinct pairs, and each of its local blocks is the row block of exactly five slots, one for each of the five offsets. Entry 0 is the row block's local index i * 2 + j of the device's 2 x 2 blocks, entry 1 the axial offset (0 or 1), entry 2 the circumferential offset (-1, 0 or 1), and an axial offset 0 comes only with a circumferential offset of 0 or 1. `pair_counts`: some device keeps all 20 slots.
All inputs are finite; a program needn't handle non-finite values.
Results may differ from the reference program's by a relative error of at most 0.0022.
Values may be sent and summed in bfloat16 or wider, within the bound.
A program may use at most 64 MiB of HBM per device.

```python
import math
import jax
import jax.numpy as jnp
from jax import lax

MODES = 512
ALONG = 16
AROUND = 8
BLK_AXIAL = 2
BLK_CIRC = 2
PAIRS_DEV = 20
NBA = 32
NBC = 4
N_AXIAL = 16
N_CIRC = 2


def draw_pair_list(key, part):
    device_total = N_AXIAL * N_CIRC
    slot_total = PAIRS_DEV
    scores = jax.random.randint(key, (device_total, slot_total), 0, 1 << 20) * slot_total + jnp.arange(slot_total, dtype=jnp.int32)[None, :]
    ordering = jnp.argsort(scores, axis=-1, stable=True).astype(jnp.int32)
    row_block = ordering // 5
    offset_kind = ordering % 5
    along_table = jnp.array([0, 0, 1, 1, 1], jnp.int32)
    around_table = jnp.array([0, 1, -1, 0, 1], jnp.int32)
    stacked = jnp.stack([row_block, along_table[offset_kind], around_table[offset_kind]], axis=1)
    return stacked.reshape(N_AXIAL, N_CIRC, 3, slot_total).astype(jnp.int32)


def draw_pair_counts(key, part):
    device_total = N_AXIAL * N_CIRC
    count_key = jax.random.fold_in(key, 11)
    spot_key = jax.random.fold_in(key, 23)
    counts_drawn = jax.random.randint(count_key, (device_total,), PAIRS_DEV // 8, PAIRS_DEV + 1)
    fullest = jax.random.randint(spot_key, (), 0, device_total)
    counts_drawn = counts_drawn.at[fullest].set(PAIRS_DEV)
    return counts_drawn.reshape(N_AXIAL, N_CIRC).astype(jnp.int32)


def spiked(result, own_key, source, target, blocks, factor):
    owner, partner = [(jnp.arange(result.shape[position]) // (result.shape[position] // blocks)).reshape([-1 if axis == position else 1 for axis in range(result.ndim)]) for position in (source, target)]
    chosen = jax.random.permutation(own_key, blocks)[partner]
    strong = (owner == chosen) | (owner == (partner + blocks // 2) % blocks)
    return jnp.where(strong, factor * result, result)


def shard_levels(own_key, dims, pieces, low, high):
    loudness, own = 1.0, jax.random.fold_in(own_key, 6)
    for axis_at, shards_of in pieces:
        steps = jnp.exp(jax.random.uniform(jax.random.fold_in(own, axis_at), (shards_of,), jnp.float32, low / len(pieces), high / len(pieces)))
        loudness = loudness * jnp.repeat(steps, dims[axis_at] // shards_of).reshape([-1 if axis == axis_at else 1 for axis in range(len(dims))])
    return loudness


def gaussian_with(rng, shape, scale, most, pieces, heavy, kind=jnp.bfloat16):
    values = scale * jax.random.normal(rng, shape, jnp.float32)
    if pieces:
        values = values * shard_levels(rng, shape, pieces, -0.22, 0.18)
    return jnp.clip(spiked(values, jax.random.fold_in(rng, 3), *heavy), -most, most).astype(kind)


def setup_inputs(seed: int = 0) -> dict:
    key_of = jax.random.split(jax.random.key(seed), 5)
    return {
        "mode_shapes": gaussian_with(key_of[0], (NBA, NBC, ALONG * AROUND, MODES), (ALONG * AROUND * NBA * NBC) ** -0.5, 0.0625, ((0, 16), (1, 2)), (0, 3, 16, 2.0), jnp.float32),
        "amplitude": jnp.clip(jnp.exp(math.log(3.0) - 2.3025851 * jax.random.uniform(key_of[1], (NBA, NBC, ALONG * AROUND), jnp.float32) ** shard_levels(key_of[1], (NBA, NBC, ALONG * AROUND), ((0, 16), (1, 2)), -0.2, 0.2)), 0.3, 3.0),
        "pair_list": draw_pair_list(jax.random.fold_in(key_of[4], 71), 0),
        "pair_counts": draw_pair_counts(jax.random.fold_in(key_of[4], 71), 0),
    }


axial_decay = 0.125
circ_decay = 0.16
wavenumber = 0.6


def corcos_tiles(step_along, step_around, weight):
    patch_index = jnp.arange(ALONG * AROUND, dtype=jnp.int32)
    along_pos = (patch_index // AROUND).astype(jnp.float32)
    around_pos = (patch_index % AROUND).astype(jnp.float32)
    gap_along = step_along.astype(jnp.float32)[:, None, None] * ALONG + along_pos[None, None, :] - along_pos[None, :, None]
    gap_around = step_around.astype(jnp.float32)[:, None, None] * AROUND + around_pos[None, None, :] - around_pos[None, :, None]
    envelope = weight[:, None, None] * jnp.exp(-axial_decay * jnp.abs(gap_along) - circ_decay * jnp.abs(gap_around))
    real_tile = envelope * jnp.cos(wavenumber * gap_along)
    imag_tile = -envelope * jnp.sin(wavenumber * gap_along)
    return jnp.stack([real_tile, imag_tile], axis=1).astype(jnp.bfloat16)


def reference(mode_shapes, amplitude, pair_list, pair_counts):
    weighted = (mode_shapes * amplitude[..., None]).astype(jnp.bfloat16)
    widened = jnp.concatenate([weighted[:, -1:], weighted, weighted[:, :1]], axis=1)
    extended = jnp.concatenate([widened, jnp.zeros((1,) + widened.shape[1:], jnp.bfloat16)], axis=0)
    block_count = BLK_AXIAL * BLK_CIRC
    patch_count = ALONG * AROUND

    def per_device(totals, device):
        along_dev = device // N_CIRC
        around_dev = device % N_CIRC
        listing = pair_list[along_dev, around_dev]
        row_block = listing[0]
        step_along = listing[1]
        step_around = listing[2]
        slot_index = jnp.arange(PAIRS_DEV, dtype=jnp.int32)
        valid = (slot_index < pair_counts[along_dev, around_dev]).astype(jnp.float32)
        weight = valid * jnp.where((step_along == 0) & (step_around == 0), 0.5, 1.0).astype(jnp.float32)
        global_along = along_dev * BLK_AXIAL + row_block // BLK_CIRC
        global_around = around_dev * BLK_CIRC + row_block % BLK_CIRC
        columns = extended[global_along + step_along, global_around + step_around + 1]
        tiles = corcos_tiles(step_along, step_around, weight)
        products = jnp.einsum("pcij,pjm->picm", tiles.astype(jnp.float32), columns.astype(jnp.float32))
        products = products.reshape(PAIRS_DEV, patch_count, 2 * MODES)
        row_sums = jax.ops.segment_sum(products, row_block, num_segments=block_count)
        rounded = row_sums.astype(jnp.bfloat16).reshape(block_count * patch_count, 2 * MODES)
        start_along = (along_dev * BLK_AXIAL).astype(jnp.int32)
        start_around = (around_dev * BLK_CIRC).astype(jnp.int32)
        zero_index = jnp.int32(0)
        local = lax.dynamic_slice(weighted, (start_along, start_around, zero_index, zero_index), (BLK_AXIAL, BLK_CIRC, patch_count, MODES))
        local = local.reshape(block_count * patch_count, MODES)
        cross = lax.dot_general(local, rounded, (((0,), (0,)), ((), ())), preferred_element_type=jnp.float32)
        return totals + cross, None

    totals, unused = lax.scan(per_device, jnp.zeros((MODES, 2 * MODES), jnp.float32), jnp.arange(N_AXIAL * N_CIRC, dtype=jnp.int32))
    real_part = totals[:, :MODES]
    imag_part = totals[:, MODES:]
    return jnp.stack([real_part + real_part.T, imag_part - imag_part.T])
```

```python
import functools

import numpy as np
import ml_dtypes
import jax
import jax.numpy as jnp
from jax import lax
from jax.experimental import pallas as pl
from jax.experimental.pallas import tpu as pltpu
from jax.sharding import PartitionSpec as P

ALONG = 16
AROUND = 8
PATCH = ALONG * AROUND
DECAY_A = 0.125
DECAY_C = 0.16
WAVE = 0.6
KINDS = ((0, 0), (0, 1), (1, -1), (1, 0), (1, 1))
HALO = 112
HALO_PAD = 128
MESH = pl.DeviceIdType.MESH


def split(values):
    high = values.astype(ml_dtypes.bfloat16)
    low = (values - high.astype(np.float64)).astype(ml_dtypes.bfloat16)
    return high, low


@functools.lru_cache(None)
def tables():
    index = np.arange(PATCH)
    along, around = index // AROUND, index % AROUND
    tiles = []
    for step_a, step_c in KINDS:
        gap_a = (step_a * ALONG + along[None, :] - along[:, None]).astype(np.float32)
        gap_c = (step_c * AROUND + around[None, :] - around[:, None]).astype(np.float32)
        weight = np.float32(0.5 if (step_a, step_c) == (0, 0) else 1.0)
        envelope = weight * np.exp(np.float32(-DECAY_A) * np.abs(gap_a) - np.float32(DECAY_C) * np.abs(gap_c))
        angle = np.float32(WAVE) * gap_a
        tiles.append(np.concatenate([envelope * np.cos(angle), -envelope * np.sin(angle)]))
    tiles = np.stack(tiles).astype(ml_dtypes.bfloat16)

    g = np.zeros((40, PATCH))
    forward = np.exp(-DECAY_C * around)
    backward = np.exp(-DECAY_C * (AROUND - around))
    phase = np.exp((-DECAY_A - 1j * WAVE) * along)
    for k in range(ALONG):
        g[k] = forward * (along == k)
    for k in range(AROUND):
        g[16 + k] = phase.real * (around == k)
        g[24 + k] = phase.imag * (around == k)
    g[32], g[33] = (phase * forward).real, (phase * forward).imag
    g[34], g[35] = (phase * backward).real, (phase * backward).imag
    gather = np.concatenate(split(g))

    spread = np.zeros((4, PATCH, HALO_PAD), np.complex128)
    code = np.full((HALO_PAD, 1), -1, np.int32)
    alpha = np.exp((-DECAY_A - 1j * WAVE) * (ALONG - along))
    ahead = np.exp(-DECAY_C * (AROUND - around))
    behind = np.exp(-DECAY_C * around)

    def around_sums(block, base):
        for k in range(ALONG):
            gap = k - along
            spread[block, :, base + k] = np.exp(-DECAY_A * np.abs(gap) - 1j * WAVE * gap) * ahead
            code[base + k] = block * 5 + 1

    def along_sums(block, base):
        for k in range(AROUND):
            value = alpha * np.exp(-DECAY_C * np.abs(k - around))
            spread[block, :, base + k] = value
            spread[block, :, base + 8 + k] = 1j * value
            code[base + k] = code[base + 8 + k] = block * 5 + 3

    def both_sums(block, base, kind):
        value = alpha * (ahead if kind == 4 else behind)
        spread[block, :, base] = value
        spread[block, :, base + 1] = 1j * value
        code[base] = code[base + 1] = block * 5 + kind

    around_sums(1, 0)
    around_sums(3, 16)
    both_sums(1, 32, 4)
    both_sums(0, 40 + 2, 2)
    along_sums(2, 48)
    both_sums(3, 48 + 18, 2)
    along_sums(3, 72)
    both_sums(2, 72 + 16, 4)
    both_sums(3, 96, 4)
    both_sums(2, 104 + 2, 2)
    spread = spread.reshape(4 * PATCH, HALO_PAD)
    spread = np.stack(split(np.concatenate([spread.real, spread.imag], axis=1)))
    return tiles, gather, spread, code


LOCAL = ((0, 1, 3, 4), (0, 2, 3), (0, 1), (0,))
MESSAGES = ((0, -1, 0, 40), (0, 1, 40, 8), (-1, 0, 48, 48), (-1, -1, 96, 8), (-1, 1, 104, 8))


def parts(value):
    high = value.astype(jnp.bfloat16)
    return high, (value - high.astype(jnp.float32)).astype(jnp.bfloat16)


def dot(a, b):
    return jnp.dot(a, b, preferred_element_type=jnp.float32)


def spectrum(axial, circ, shapes_ref, amp_ref, list_ref, count_ref, tiles_ref, gather_ref, spread_ref, code_ref,
             halo_out, halo_in, halo_send, halo_recv, weighted, relations):
    a, c = lax.axis_index("axial"), lax.axis_index("circ")
    modes = shapes_ref.shape[-1]

    def device(step_a, step_c):
        return (lax.rem(a + step_a + axial, axial), lax.rem(c + step_c + circ, circ))

    halo_in[...] = jnp.zeros_like(halo_in)
    barrier = pltpu.get_barrier_semaphore()
    greeted = [device(sa, sc) for sa, sc, _, _ in MESSAGES] + [device(-sa, -sc) for sa, sc, _, _ in MESSAGES] + relations
    for target in greeted:
        pl.semaphore_signal(barrier, inc=1, device_id=target, device_id_type=MESH)

    sums = []
    for block in range(4):
        i, j = block // 2, block % 2
        column = jnp.broadcast_to(amp_ref[i, j : j + 1, :], (PATCH, PATCH)).T
        wide = jnp.concatenate([column] * (modes // PATCH), axis=1)
        weighted[block * PATCH : (block + 1) * PATCH, :] = (shapes_ref[i, j] * wide).astype(jnp.bfloat16)
        both = dot(gather_ref[...], weighted[block * PATCH : (block + 1) * PATCH, :])
        sums.append(both[:40] + both[40:])
    halo_out[0:16] = sums[0][0:16]
    halo_out[16:32] = sums[2][0:16]
    halo_out[32:40] = sums[2][32:40]
    halo_out[40:48] = sums[3][32:40]
    halo_out[48:72] = sums[0][16:40]
    halo_out[72:96] = sums[1][16:40]
    halo_out[96:104] = sums[0][32:40]
    halo_out[104:112] = sums[1][32:40]
    pl.semaphore_wait(barrier, len(greeted))

    def copy_of(at):
        step_a, step_c, base, rows = MESSAGES[at]
        return pltpu.make_async_remote_copy(
            src_ref=halo_out.at[pl.ds(base, rows)],
            dst_ref=halo_in.at[pl.ds(base, rows)],
            send_sem=halo_send.at[at],
            recv_sem=halo_recv.at[at],
            device_id=device(step_a, step_c),
            device_id_type=MESH,
        )

    for at in range(2):
        copy_of(at).start()

    @pl.when(a > 0)
    def _():
        for at in range(2, 5):
            copy_of(at).start()

    listing = list_ref[0, 0]
    slot_code = listing[0:1] * 5 + listing[1:2] * 3 + listing[2:3]
    kept = lax.broadcasted_iota(jnp.int32, slot_code.shape, 1) < count_ref[...]
    slot_code = jnp.where(kept, slot_code, -2)
    wanted = lax.broadcasted_iota(jnp.int32, (24, slot_code.shape[1]), 0)
    weights = jnp.sum(jnp.where(wanted == slot_code, 1.0, 0.0), axis=1, keepdims=True)
    halo_weights = jnp.sum(jnp.where(code_ref[...] == slot_code, 1.0, 0.0), axis=1, keepdims=True)

    real_sums, imag_sums = [], []
    for block in range(4):
        tiles = []
        for kind in LOCAL[block]:
            at = block * 5 + kind
            tiles.append(tiles_ref[kind] * jnp.broadcast_to(weights[at : at + 1], (2 * PATCH, PATCH)).astype(jnp.bfloat16))
        tile = tiles[0] if len(tiles) == 1 else jnp.concatenate(tiles, axis=1)
        total = dot(tile, weighted[(4 - len(tiles)) * PATCH :, :])
        real_sums.append(total[:PATCH])
        imag_sums.append(total[PATCH:])
    turned = weighted[...].T
    real_high, real_low = parts(jnp.concatenate(real_sums, axis=0))
    imag_high, imag_low = parts(jnp.concatenate(imag_sums, axis=0))
    real_cross = dot(turned, real_high) + dot(turned, real_low)
    imag_cross = dot(turned, imag_high) + dot(turned, imag_low)
    through = dot(turned, spread_ref[0]) + dot(turned, spread_ref[1])
    high, low = parts(through)
    real_left = jnp.concatenate([x[:, :HALO_PAD] for x in (high, low, high)], axis=1)
    imag_left = jnp.concatenate([x[:, HALO_PAD:] for x in (high, low, high)], axis=1)

    for at in range(2):
        copy_of(at).wait_recv()

    @pl.when(a < axial - 1)
    def _():
        for at in range(2, 5):
            copy_of(at).wait_recv()

    received_high, received_low = parts(halo_in[...] * halo_weights)
    right = jnp.concatenate([received_high, received_high, received_low], axis=0)
    real_cross = real_cross + dot(real_left, right)
    imag_cross = imag_cross + dot(imag_left, right)

    for at in range(2):
        copy_of(at).wait_send()

    @pl.when(a > 0)
    def _():
        for at in range(2, 5):
            copy_of(at).wait_send()

    return real_cross + real_cross.T, imag_cross - imag_cross.T


def plain_kernel(axial, circ, shapes_ref, amp_ref, list_ref, count_ref, tiles_ref, gather_ref, spread_ref, code_ref, out_ref,
                 halo_out, halo_in, halo_send, halo_recv, weighted):
    real, imag = spectrum(axial, circ, shapes_ref, amp_ref, list_ref, count_ref, tiles_ref, gather_ref, spread_ref, code_ref,
                          halo_out, halo_in, halo_send, halo_recv, weighted, [])
    out_ref[0] = real
    out_ref[1] = imag


def full_kernel(axial, circ, shapes_ref, amp_ref, list_ref, count_ref, tiles_ref, gather_ref, spread_ref, code_ref, out_ref,
                halo_out, halo_in, halo_send, halo_recv, weighted,
                pieces, recv0, recv1, recv2, recv3, send_sem, recv_sem):
    a, c = lax.axis_index("axial"), lax.axis_index("circ")
    depth = axial // 4
    core, y, z = lax.rem(a, 2), lax.rem(a // 2, 2), a // 4
    flip_core = (a + 1 - 2 * core, c)
    first_a = a + core * (2 - 4 * y)
    first_c = c + (1 - core) * (1 - 2 * c)
    second_a = a + (1 - core) * (2 - 4 * y)
    second_c = c + core * (1 - 2 * c)
    key1 = core * y + (1 - core) * c
    key2 = core * c + (1 - core) * y
    slices = [(lax.rem(z + d, depth) * 4 + lax.rem(a, 4), c) for d in range(1, depth)]
    relations = [flip_core, (first_a, first_c), (second_a, second_c)] + slices

    real, imag = spectrum(axial, circ, shapes_ref, amp_ref, list_ref, count_ref, tiles_ref, gather_ref, spread_ref, code_ref,
                          halo_out, halo_in, halo_send, halo_recv, weighted, relations)
    rows, columns = real.shape[0] // axial, real.shape[1] // circ
    for to_core in range(2):
        for to_y in range(2):
            for to_x in range(2):
                for to_z in range(depth):
                    start = (to_z * 4 + to_y * 2 + to_core) * rows
                    place = (to_core,) + ((to_x, to_y) if to_core == 0 else (to_y, to_x)) + (to_z,)
                    for part, value in enumerate((real, imag)):
                        pieces[place + (part,)] = value[start : start + rows, to_x * columns : (to_x + 1) * columns]

    def send(source, target, at, device):
        copy = pltpu.make_async_remote_copy(
            src_ref=source, dst_ref=target, send_sem=send_sem.at[at], recv_sem=recv_sem.at[at], device_id=device, device_id_type=MESH
        )
        copy.start()
        return copy

    copies = [send(pieces.at[1 - core], recv0, 0, flip_core)]
    copies[0].wait_recv()
    recv0[1 - key1] = recv0[1 - key1] + pieces[core, 1 - key1]
    copies.append(send(recv0.at[1 - key1], recv1, 1, (first_a, first_c)))
    own = recv0[key1] + pieces[core, key1]
    recv0[key1] = own
    copies[1].wait_recv()
    recv1[1 - key2] = recv1[1 - key2] + recv0[key1, 1 - key2]
    copies.append(send(recv1.at[1 - key2], recv2, 2, (second_a, second_c)))
    recv1[key2] = recv1[key2] + recv0[key1, key2]
    copies[2].wait_recv()
    recv2[...] = recv2[...] + recv1[key2]
    for d in range(1, depth):
        copies.append(send(recv2.at[lax.rem(z + d, depth)], recv3.at[d - 1], 2 + d, slices[d - 1]))
    total = recv2[z]
    for d in range(1, depth):
        copies[2 + d].wait_recv()
        total = total + recv3[d - 1]
    out_ref[...] = total
    for copy in copies:
        copy.wait_send()


def solution(mesh):
    axial, circ = mesh.shape["axial"], mesh.shape["circ"]

    def body(mode_shapes, amplitude, pair_list, pair_counts):
        modes = mode_shapes.shape[-1]
        constants = tables()
        rows, columns = modes // axial, modes // circ
        vmem = pl.BlockSpec(memory_space=pltpu.VMEM)
        scratch = [
            pltpu.VMEM((HALO, modes), jnp.float32),
            pltpu.VMEM((HALO_PAD, modes), jnp.float32),
            pltpu.SemaphoreType.DMA((5,)),
            pltpu.SemaphoreType.DMA((5,)),
            pltpu.VMEM((4 * PATCH, modes), jnp.bfloat16),
        ]
        together = circ == 2 and axial % 4 == 0 and rows % 8 == 0 and columns % 128 == 0
        depth = axial // 4
        if together:
            kernel, shape = full_kernel, (2, rows, columns)
            piece = (depth, 2, rows, columns)
            scratch += [
                pltpu.VMEM((2, 2, 2) + piece, jnp.float32),
                pltpu.VMEM((2, 2) + piece, jnp.float32),
                pltpu.VMEM((2,) + piece, jnp.float32),
                pltpu.VMEM(piece, jnp.float32),
                pltpu.VMEM((depth - 1,) + piece[1:], jnp.float32),
                pltpu.SemaphoreType.DMA((2 + depth,)),
                pltpu.SemaphoreType.DMA((2 + depth,)),
            ]
        else:
            kernel, shape = plain_kernel, (2, modes, modes)
        result = pl.pallas_call(
            functools.partial(kernel, axial, circ),
            out_shape=jax.ShapeDtypeStruct(shape, jnp.float32),
            in_specs=[vmem] * 8,
            out_specs=vmem,
            scratch_shapes=scratch,
            compiler_params=pltpu.CompilerParams(collective_id=0, has_side_effects=True, vmem_limit_bytes=40 * 1024 * 1024),
        )(mode_shapes, amplitude, pair_list, pair_counts, *constants)
        if not together:
            result = lax.psum_scatter(result, "axial", scatter_dimension=1, tiled=True)
            result = lax.psum_scatter(result, "circ", scatter_dimension=2, tiled=True)
        return result

    in_specs = (
        P("axial", "circ", None, None),
        P("axial", "circ", None),
        P("axial", "circ", None, None),
        P("axial", "circ"),
    )
    return jax.shard_map(body, mesh=mesh, in_specs=in_specs, out_specs=P(None, "axial", "circ"), check_vma=False)
```

```python
import functools

import numpy as np
import ml_dtypes
import jax
import jax.numpy as jnp
from jax import lax
from jax.experimental import pallas as pl
from jax.experimental.pallas import tpu as pltpu
from jax.sharding import PartitionSpec as P

ALONG = 16
AROUND = 8
PATCH = ALONG * AROUND
DECAY_A = 0.125
DECAY_C = 0.16
WAVE = 0.6
KINDS = ((0, 0), (0, 1), (1, -1), (1, 0), (1, 1))
HALO = 112
HALO_PAD = 128
LIMIT = 32767.0
MESH = pl.DeviceIdType.MESH


def split(values):
    high = values.astype(ml_dtypes.bfloat16)
    low = (values - high.astype(np.float64)).astype(ml_dtypes.bfloat16)
    return high, low


@functools.lru_cache(None)
def tables():
    index = np.arange(PATCH)
    along, around = index // AROUND, index % AROUND
    tiles = []
    for step_a, step_c in KINDS:
        gap_a = (step_a * ALONG + along[None, :] - along[:, None]).astype(np.float32)
        gap_c = (step_c * AROUND + around[None, :] - around[:, None]).astype(np.float32)
        weight = np.float32(0.5 if (step_a, step_c) == (0, 0) else 1.0)
        envelope = weight * np.exp(np.float32(-DECAY_A) * np.abs(gap_a) - np.float32(DECAY_C) * np.abs(gap_c))
        angle = np.float32(WAVE) * gap_a
        tiles.append(np.concatenate([envelope * np.cos(angle), -envelope * np.sin(angle)]))
    tiles = np.stack(tiles).astype(ml_dtypes.bfloat16)

    g = np.zeros((40, PATCH))
    forward = np.exp(-DECAY_C * around)
    backward = np.exp(-DECAY_C * (AROUND - around))
    phase = np.exp((-DECAY_A - 1j * WAVE) * along)
    for k in range(ALONG):
        g[k] = forward * (along == k)
    for k in range(AROUND):
        g[16 + k] = phase.real * (around == k)
        g[24 + k] = phase.imag * (around == k)
    g[32], g[33] = (phase * forward).real, (phase * forward).imag
    g[34], g[35] = (phase * backward).real, (phase * backward).imag
    gather = np.concatenate(split(g))

    spread = np.zeros((4, PATCH, HALO_PAD), np.complex128)
    code = np.full((HALO_PAD, 1), -1, np.int32)
    alpha = np.exp((-DECAY_A - 1j * WAVE) * (ALONG - along))
    ahead = np.exp(-DECAY_C * (AROUND - around))
    behind = np.exp(-DECAY_C * around)

    def around_sums(block, base):
        for k in range(ALONG):
            gap = k - along
            spread[block, :, base + k] = np.exp(-DECAY_A * np.abs(gap) - 1j * WAVE * gap) * ahead
            code[base + k] = block * 5 + 1

    def along_sums(block, base):
        for k in range(AROUND):
            value = alpha * np.exp(-DECAY_C * np.abs(k - around))
            spread[block, :, base + k] = value
            spread[block, :, base + 8 + k] = 1j * value
            code[base + k] = code[base + 8 + k] = block * 5 + 3

    def both_sums(block, base, kind):
        value = alpha * (ahead if kind == 4 else behind)
        spread[block, :, base] = value
        spread[block, :, base + 1] = 1j * value
        code[base] = code[base + 1] = block * 5 + kind

    around_sums(1, 0)
    around_sums(3, 16)
    both_sums(1, 32, 4)
    both_sums(0, 40 + 2, 2)
    along_sums(2, 48)
    both_sums(3, 48 + 18, 2)
    along_sums(3, 72)
    both_sums(2, 72 + 16, 4)
    both_sums(3, 96, 4)
    both_sums(2, 104 + 2, 2)
    spread = spread.reshape(4 * PATCH, HALO_PAD)
    spread = np.stack(split(np.concatenate([spread.real, spread.imag], axis=1)))
    return tiles, gather, spread, code


LOCAL = ((0, 1, 3, 4), (0, 2, 3), (0, 1), (0,))
MESSAGES = ((0, -1, 0, 40), (0, 1, 40, 8), (-1, 0, 48, 48), (-1, -1, 96, 8), (-1, 1, 104, 8))


def parts(value):
    high = value.astype(jnp.bfloat16)
    return high, (value - high.astype(jnp.float32)).astype(jnp.bfloat16)


def dot(a, b):
    return jnp.dot(a, b, preferred_element_type=jnp.float32)


def spectrum(axial, circ, operands, scratch, relations, deliver):
    shapes_hbm, amp_ref, list_ref, count_ref, tiles_hbm, gather_hbm, spread_hbm, code_ref = operands
    halo_out, halo_in, halo_send, halo_recv, weighted, shapes_ref, tiles_ref, gather_ref, spread_ref, fetch_sem = scratch
    fetches = [
        pltpu.make_async_copy(source, target, fetch_sem.at[at])
        for at, (source, target) in enumerate(
            [(gather_hbm, gather_ref)]
            + [(shapes_hbm.at[block // 2, block % 2], shapes_ref.at[block // 2, block % 2]) for block in range(4)]
            + [(tiles_hbm, tiles_ref), (spread_hbm, spread_ref)]
        )
    ]
    for fetch in fetches:
        fetch.start()
    a, c = lax.axis_index("axial"), lax.axis_index("circ")
    modes = weighted.shape[-1]

    def device(step_a, step_c):
        return (lax.rem(a + step_a + axial, axial), lax.rem(c + step_c + circ, circ))

    halo_in[...] = jnp.zeros_like(halo_in)
    barrier = pltpu.get_barrier_semaphore()
    greeted = [device(sa, sc) for sa, sc, _, _ in MESSAGES] + [device(-sa, -sc) for sa, sc, _, _ in MESSAGES] + relations
    for target in greeted:
        pl.semaphore_signal(barrier, inc=1, device_id=target, device_id_type=MESH)

    sums = []
    fetches[0].wait()
    for block in range(4):
        fetches[1 + block].wait()
        i, j = block // 2, block % 2
        column = jnp.broadcast_to(amp_ref[i, j : j + 1, :], (PATCH, PATCH)).T
        wide = jnp.concatenate([column] * (modes // PATCH), axis=1)
        weighted[block * PATCH : (block + 1) * PATCH, :] = (shapes_ref[i, j] * wide).astype(jnp.bfloat16)
        both = dot(gather_ref[...], weighted[block * PATCH : (block + 1) * PATCH, :])
        sums.append(both[:40] + both[40:])
    halo_out[0:16] = sums[0][0:16]
    halo_out[16:32] = sums[2][0:16]
    halo_out[32:40] = sums[2][32:40]
    halo_out[40:48] = sums[3][32:40]
    halo_out[48:72] = sums[0][16:40]
    halo_out[72:96] = sums[1][16:40]
    halo_out[96:104] = sums[0][32:40]
    halo_out[104:112] = sums[1][32:40]
    pl.semaphore_wait(barrier, len(greeted))

    def copy_of(at):
        step_a, step_c, base, rows = MESSAGES[at]
        return pltpu.make_async_remote_copy(
            src_ref=halo_out.at[pl.ds(base, rows)],
            dst_ref=halo_in.at[pl.ds(base, rows)],
            send_sem=halo_send.at[at],
            recv_sem=halo_recv.at[at],
            device_id=device(step_a, step_c),
            device_id_type=MESH,
        )

    for at in range(2):
        copy_of(at).start()

    @pl.when(a > 0)
    def _():
        for at in range(2, 5):
            copy_of(at).start()

    slot_code = list_ref[0] * 5 + list_ref[1] * 3 + list_ref[2]
    kept = lax.broadcasted_iota(jnp.int32, slot_code.shape, 1) < count_ref[...]
    slot_code = jnp.where(kept, slot_code, -2)
    wanted = lax.broadcasted_iota(jnp.int32, (24, slot_code.shape[1]), 0)
    weights = jnp.sum(jnp.where(wanted == slot_code, 1.0, 0.0), axis=1, keepdims=True)
    halo_weights = jnp.sum(jnp.where(code_ref[...] == slot_code, 1.0, 0.0), axis=1, keepdims=True)

    fetches[5].wait()
    real_sums, imag_sums = [], []
    for block in range(4):
        tiles = []
        for kind in LOCAL[block]:
            at = block * 5 + kind
            tiles.append(tiles_ref[kind] * jnp.broadcast_to(weights[at : at + 1], (2 * PATCH, PATCH)).astype(jnp.bfloat16))
        tile = tiles[0] if len(tiles) == 1 else jnp.concatenate(tiles, axis=1)
        total = dot(tile, weighted[(4 - len(tiles)) * PATCH :, :])
        real_sums.append(total[:PATCH])
        imag_sums.append(total[PATCH:])
    turned = weighted[...].T
    real_high, real_low = parts(jnp.concatenate(real_sums, axis=0))
    imag_high, imag_low = parts(jnp.concatenate(imag_sums, axis=0))
    real_cross = dot(turned, real_high) + dot(turned, real_low)
    imag_cross = dot(turned, imag_high) + dot(turned, imag_low)
    fetches[6].wait()
    through = dot(turned, spread_ref[0]) + dot(turned, spread_ref[1])
    high, low = parts(through)
    real_left = jnp.concatenate([x[:, :HALO_PAD] for x in (high, low, high)], axis=1)
    imag_left = jnp.concatenate([x[:, HALO_PAD:] for x in (high, low, high)], axis=1)

    for at in range(2):
        copy_of(at).wait_recv()

    @pl.when(a < axial - 1)
    def _():
        for at in range(2, 5):
            copy_of(at).wait_recv()

    received_high, received_low = parts(halo_in[...] * halo_weights)
    right = jnp.concatenate([received_high, received_high, received_low], axis=0)
    real_cross = real_cross + dot(real_left, right)
    deliver(0, real_cross + real_cross.T)
    imag_cross = imag_cross + dot(imag_left, right)
    deliver(1, imag_cross - imag_cross.T)

    for at in range(2):
        copy_of(at).wait_send()

    @pl.when(a > 0)
    def _():
        for at in range(2, 5):
            copy_of(at).wait_send()


def plain_kernel(axial, circ, *refs):
    out_ref = refs[8]

    def deliver(part, value):
        out_ref[part] = value

    spectrum(axial, circ, refs[:8], refs[9:], [], deliver)


def coded(read, write, count):
    most = None
    for at in range(count):
        value = jnp.max(jnp.abs(read(at)), axis=0, keepdims=True)
        most = value if most is None else jnp.maximum(most, value)
    most = jnp.maximum(most, 1e-30)
    factor = LIMIT / most
    for at in range(count):
        write(at, jnp.round(read(at) * factor).astype(jnp.int32).astype(jnp.int16))
    return jnp.broadcast_to(most * (1.0 / LIMIT), (8, most.shape[1]))


def decoded(value, scales):
    return value.astype(jnp.int32).astype(jnp.float32) * scales[0:1]


def full_kernel(axial, circ, *refs):
    operands, out_ref, scratch = refs[:8], refs[8], refs[9:19]
    pieces, sent, came, sent_scale, came_scale, send_sem, recv_sem = refs[19:]
    a, c = lax.axis_index("axial"), lax.axis_index("circ")
    depth = axial // 4
    core, y, z = lax.rem(a, 2), lax.rem(a // 2, 2), a // 4
    flip_core = (a + 1 - 2 * core, c)
    first = (a + core * (2 - 4 * y), c + (1 - core) * (1 - 2 * c))
    second = (a + (1 - core) * (2 - 4 * y), c + core * (1 - 2 * c))
    key1 = core * y + (1 - core) * c
    key2 = core * c + (1 - core) * y
    slices = [(lax.rem(z + d, depth) * 4 + lax.rem(a, 4), c) for d in range(1, depth)]
    rows, columns = out_ref.shape[1:]
    base = (0, 4 * depth, 6 * depth) + tuple(7 * depth + d for d in range(depth - 1))
    copies = {}

    def send(part, step, read, count, device):
        def write(at, value):
            sent[part, base[step] + at] = value

        sent_scale[part, step] = coded(read, write, count)
        span = pl.ds(base[step], count)
        for at, (source, target) in enumerate(
            ((sent.at[part, span], came.at[part, span]), (sent_scale.at[part, step], came_scale.at[part, step]))
        ):
            copy = pltpu.make_async_remote_copy(
                src_ref=source,
                dst_ref=target,
                send_sem=send_sem.at[part, step, at],
                recv_sem=recv_sem.at[part, step, at],
                device_id=device,
                device_id_type=MESH,
            )
            copy.start()
            copies[part, step, at] = copy

    def receive(part, step):
        for at in range(2):
            copies[part, step, at].wait_recv()
        return came_scale[part, step]

    def deliver(part, value):
        for to_core in range(2):
            for to_y in range(2):
                for to_x in range(2):
                    for to_z in range(depth):
                        start = (to_z * 4 + to_y * 2 + to_core) * rows
                        place = (to_core,) + ((to_x, to_y) if to_core == 0 else (to_y, to_x))
                        at = ((place[0] * 2 + place[1]) * 2 + place[2]) * depth + to_z
                        pieces[part, at] = value[start : start + rows, to_x * columns : (to_x + 1) * columns]
        other = (1 - core) * 4 * depth
        send(part, 0, lambda at: pieces[part, other + at], 4 * depth, flip_core)

    spectrum(axial, circ, operands, scratch, [flip_core, first, second] + slices, deliver)

    def add(part, step, scales, own, offset, count):
        for at in range(count):
            pieces[part, own + offset + at] += decoded(came[part, base[step] + offset + at], scales)

    for part in range(2):
        scales = receive(part, 0)
        own, give, keep = core * 4 * depth, (1 - key1) * 2 * depth, key1 * 2 * depth
        add(part, 0, scales, own, give, 2 * depth)
        send(part, 1, lambda at: pieces[part, own + give + at], 2 * depth, first)
        add(part, 0, scales, own, keep, 2 * depth)
    for part in range(2):
        scales = receive(part, 1)
        own, give, keep = core * 4 * depth + key1 * 2 * depth, (1 - key2) * depth, key2 * depth
        add(part, 1, scales, own, give, depth)
        send(part, 2, lambda at: pieces[part, own + give + at], depth, second)
        add(part, 1, scales, own, keep, depth)
    for part in range(2):
        scales = receive(part, 2)
        own = core * 4 * depth + key1 * 2 * depth + key2 * depth
        add(part, 2, scales, own, 0, depth)
        for d in range(1, depth):
            send(part, 2 + d, lambda at: pieces[part, own + lax.rem(z + d, depth)], 1, slices[d - 1])
    for part in range(2):
        total = pieces[part, own + z]
        for d in range(1, depth):
            scales = receive(part, 2 + d)
            total = total + decoded(came[part, base[2 + d]], scales)
        out_ref[part] = total
    for copy in copies.values():
        copy.wait_send()


def solution(mesh):
    axial, circ = mesh.shape["axial"], mesh.shape["circ"]

    def body(mode_shapes, amplitude, pair_list, pair_counts):
        modes = mode_shapes.shape[-1]
        constants = tables()
        rows, columns = modes // axial, modes // circ
        vmem, hbm = pl.BlockSpec(memory_space=pltpu.VMEM), pl.BlockSpec(memory_space=pltpu.HBM)
        scratch = [
            pltpu.VMEM((HALO, modes), jnp.float32),
            pltpu.VMEM((HALO_PAD, modes), jnp.float32),
            pltpu.SemaphoreType.DMA((5,)),
            pltpu.SemaphoreType.DMA((5,)),
            pltpu.VMEM((4 * PATCH, modes), jnp.bfloat16),
            pltpu.VMEM(mode_shapes.shape, jnp.float32),
        ]
        scratch += [pltpu.VMEM(value.shape, jnp.bfloat16) for value in constants[:3]]
        scratch.append(pltpu.SemaphoreType.DMA((7,)))
        together = circ == 2 and axial % 4 == 0 and rows % 32 == 0 and columns % 128 == 0
        depth = axial // 4
        if together:
            kernel, shape = full_kernel, (2, rows, columns)
            steps, total = 2 + depth, 8 * depth
            scratch += [
                pltpu.VMEM((2, 8 * depth, rows, columns), jnp.float32),
                pltpu.VMEM((2, total, rows, columns), jnp.int16),
                pltpu.VMEM((2, total, rows, columns), jnp.int16),
                pltpu.VMEM((2, steps, 8, columns), jnp.float32),
                pltpu.VMEM((2, steps, 8, columns), jnp.float32),
                pltpu.SemaphoreType.DMA((2, steps, 2)),
                pltpu.SemaphoreType.DMA((2, steps, 2)),
            ]
        else:
            kernel, shape = plain_kernel, (2, modes, modes)
        result = pl.pallas_call(
            functools.partial(kernel, axial, circ),
            out_shape=jax.ShapeDtypeStruct(shape, jnp.float32),
            in_specs=[hbm] + [vmem] * 3 + [hbm] * 3 + [vmem],
            out_specs=vmem,
            scratch_shapes=scratch,
            compiler_params=pltpu.CompilerParams(collective_id=0, has_side_effects=True, vmem_limit_bytes=56 * 1024 * 1024),
        )(mode_shapes, amplitude, pair_list.reshape(3, 1, -1), pair_counts, *constants)
        if not together:
            result = lax.psum_scatter(result, "axial", scatter_dimension=1, tiled=True)
            result = lax.psum_scatter(result, "circ", scatter_dimension=2, tiled=True)
        return result

    in_specs = (
        P("axial", "circ", None, None),
        P("axial", "circ", None),
        P("axial", "circ", None, None),
        P("axial", "circ"),
    )
    return jax.shard_map(body, mesh=mesh, in_specs=in_specs, out_specs=P(None, "axial", "circ"), check_vma=False)
```

```python
import functools

import numpy as np
import ml_dtypes
import jax
import jax.numpy as jnp
from jax import lax
from jax.experimental import pallas as pl
from jax.experimental.pallas import tpu as pltpu
from jax.sharding import PartitionSpec as P

ALONG = 16
AROUND = 8
PATCH = ALONG * AROUND
DECAY_A = 0.125
DECAY_C = 0.16
WAVE = 0.6
KINDS = ((0, 0), (0, 1), (1, -1), (1, 0), (1, 1))
HALO = 112
HALO_PAD = 128
LIMIT = 32767.0
MESH = pl.DeviceIdType.MESH


def split(values):
    high = values.astype(ml_dtypes.bfloat16)
    low = (values - high.astype(np.float64)).astype(ml_dtypes.bfloat16)
    return high, low


@functools.lru_cache(None)
def tables():
    index = np.arange(PATCH)
    along, around = index // AROUND, index % AROUND
    tiles = []
    for step_a, step_c in KINDS:
        gap_a = (step_a * ALONG + along[None, :] - along[:, None]).astype(np.float32)
        gap_c = (step_c * AROUND + around[None, :] - around[:, None]).astype(np.float32)
        weight = np.float32(0.5 if (step_a, step_c) == (0, 0) else 1.0)
        envelope = weight * np.exp(np.float32(-DECAY_A) * np.abs(gap_a) - np.float32(DECAY_C) * np.abs(gap_c))
        angle = np.float32(WAVE) * gap_a
        tiles.append(np.concatenate([envelope * np.cos(angle), -envelope * np.sin(angle)]))
    tiles = np.stack(tiles).astype(ml_dtypes.bfloat16)

    g = np.zeros((40, PATCH))
    forward = np.exp(-DECAY_C * around)
    backward = np.exp(-DECAY_C * (AROUND - around))
    phase = np.exp((-DECAY_A - 1j * WAVE) * along)
    for k in range(ALONG):
        g[k] = forward * (along == k)
    for k in range(AROUND):
        g[16 + k] = phase.real * (around == k)
        g[24 + k] = phase.imag * (around == k)
    g[32], g[33] = (phase * forward).real, (phase * forward).imag
    g[34], g[35] = (phase * backward).real, (phase * backward).imag
    gather = np.concatenate(split(g))

    spread = np.zeros((4, PATCH, HALO_PAD), np.complex128)
    code = np.full((HALO_PAD, 1), -1, np.int32)
    alpha = np.exp((-DECAY_A - 1j * WAVE) * (ALONG - along))
    ahead = np.exp(-DECAY_C * (AROUND - around))
    behind = np.exp(-DECAY_C * around)

    def around_sums(block, base):
        for k in range(ALONG):
            gap = k - along
            spread[block, :, base + k] = np.exp(-DECAY_A * np.abs(gap) - 1j * WAVE * gap) * ahead
            code[base + k] = block * 5 + 1

    def along_sums(block, base):
        for k in range(AROUND):
            value = alpha * np.exp(-DECAY_C * np.abs(k - around))
            spread[block, :, base + k] = value
            spread[block, :, base + 8 + k] = 1j * value
            code[base + k] = code[base + 8 + k] = block * 5 + 3

    def both_sums(block, base, kind):
        value = alpha * (ahead if kind == 4 else behind)
        spread[block, :, base] = value
        spread[block, :, base + 1] = 1j * value
        code[base] = code[base + 1] = block * 5 + kind

    around_sums(1, 0)
    around_sums(3, 16)
    both_sums(1, 32, 4)
    both_sums(0, 40 + 2, 2)
    along_sums(2, 48)
    both_sums(3, 48 + 18, 2)
    along_sums(3, 72)
    both_sums(2, 72 + 16, 4)
    both_sums(3, 96, 4)
    both_sums(2, 104 + 2, 2)
    spread = spread.reshape(4 * PATCH, HALO_PAD)
    spread = np.stack(split(np.concatenate([spread.real, spread.imag], axis=1)))
    return tiles, gather, spread, code


LOCAL = ((0, 1, 3, 4), (0, 2, 3), (0, 1), (0,))
MESSAGES = ((0, -1, 0, 40), (0, 1, 40, 8), (-1, 0, 48, 48), (-1, -1, 96, 8), (-1, 1, 104, 8))


def parts(value):
    high = value.astype(jnp.bfloat16)
    return high, (value - high.astype(jnp.float32)).astype(jnp.bfloat16)


def dot(a, b):
    return jnp.dot(a, b, preferred_element_type=jnp.float32)


def spectrum(axial, circ, operands, scratch, relations, deliver):
    shapes_hbm, amp_hbm, list_hbm, count_hbm, tiles_hbm, gather_hbm, spread_hbm, code_hbm = operands
    halo_out, halo_in, halo_send, halo_recv, weighted, shapes_ref, tiles_ref, gather_ref, spread_ref, amp_ref, list_ref, count_ref, code_ref, fetch_sem = scratch
    fetches = [
        pltpu.make_async_copy(source, target, fetch_sem.at[at])
        for at, (source, target) in enumerate(
            [(gather_hbm, gather_ref)]
            + [(shapes_hbm.at[block // 2, block % 2], shapes_ref.at[block // 2, block % 2]) for block in range(4)]
            + [(tiles_hbm, tiles_ref), (spread_hbm, spread_ref)]
            + [(amp_hbm, amp_ref), (list_hbm, list_ref), (count_hbm, count_ref), (code_hbm, code_ref)]
        )
    ]
    for fetch in fetches:
        fetch.start()
    a, c = lax.axis_index("axial"), lax.axis_index("circ")
    modes = weighted.shape[-1]

    def device(step_a, step_c):
        return (lax.rem(a + step_a + axial, axial), lax.rem(c + step_c + circ, circ))

    halo_in[...] = jnp.zeros_like(halo_in)
    barrier = pltpu.get_barrier_semaphore()
    steps = {(s * sa, s * sc % circ) for sa, sc, _, _ in MESSAGES for s in (1, -1)}
    greeted = [device(sa, sc) for sa, sc in sorted(steps)] + relations
    for target in greeted:
        pl.semaphore_signal(barrier, inc=1, device_id=target, device_id_type=MESH)

    sums = []
    fetches[0].wait()
    fetches[7].wait()
    for block in range(4):
        fetches[1 + block].wait()
        i, j = block // 2, block % 2
        column = jnp.broadcast_to(amp_ref[i, j : j + 1, :], (PATCH, PATCH)).T
        wide = jnp.concatenate([column] * (modes // PATCH), axis=1)
        weighted[block * PATCH : (block + 1) * PATCH, :] = (shapes_ref[i, j] * wide).astype(jnp.bfloat16)
        both = dot(gather_ref[...], weighted[block * PATCH : (block + 1) * PATCH, :])
        sums.append(both[:40] + both[40:])
    halo_out[0:16] = sums[0][0:16]
    halo_out[16:32] = sums[2][0:16]
    halo_out[32:40] = sums[2][32:40]
    halo_out[40:48] = sums[3][32:40]
    halo_out[48:72] = sums[0][16:40]
    halo_out[72:96] = sums[1][16:40]
    halo_out[96:104] = sums[0][32:40]
    halo_out[104:112] = sums[1][32:40]
    pl.semaphore_wait(barrier, len(greeted))

    def copy_of(at):
        step_a, step_c, base, rows = MESSAGES[at]
        return pltpu.make_async_remote_copy(
            src_ref=halo_out.at[pl.ds(base, rows)],
            dst_ref=halo_in.at[pl.ds(base, rows)],
            send_sem=halo_send.at[at],
            recv_sem=halo_recv.at[at],
            device_id=device(step_a, step_c),
            device_id_type=MESH,
        )

    for at in range(2):
        copy_of(at).start()

    @pl.when(a > 0)
    def _():
        for at in range(2, 5):
            copy_of(at).start()

    for at in range(8, 11):
        fetches[at].wait()
    slot_code = list_ref[0] * 5 + list_ref[1] * 3 + list_ref[2]
    kept = lax.broadcasted_iota(jnp.int32, slot_code.shape, 1) < count_ref[...]
    slot_code = jnp.where(kept, slot_code, -2)
    wanted = lax.broadcasted_iota(jnp.int32, (24, slot_code.shape[1]), 0)
    weights = jnp.sum(jnp.where(wanted == slot_code, 1.0, 0.0), axis=1, keepdims=True)
    halo_weights = jnp.sum(jnp.where(code_ref[...] == slot_code, 1.0, 0.0), axis=1, keepdims=True)

    fetches[5].wait()
    real_sums, imag_sums = [], []
    for block in range(4):
        tiles = []
        for kind in LOCAL[block]:
            at = block * 5 + kind
            tiles.append(tiles_ref[kind] * jnp.broadcast_to(weights[at : at + 1], (2 * PATCH, PATCH)).astype(jnp.bfloat16))
        tile = tiles[0] if len(tiles) == 1 else jnp.concatenate(tiles, axis=1)
        total = dot(tile, weighted[(4 - len(tiles)) * PATCH :, :])
        real_sums.append(total[:PATCH])
        imag_sums.append(total[PATCH:])
    turned = weighted[...].T
    real_high, real_low = parts(jnp.concatenate(real_sums, axis=0))
    imag_high, imag_low = parts(jnp.concatenate(imag_sums, axis=0))
    real_cross = dot(turned, real_high) + dot(turned, real_low)
    imag_cross = dot(turned, imag_high) + dot(turned, imag_low)
    fetches[6].wait()
    through = dot(turned, spread_ref[0]) + dot(turned, spread_ref[1])
    high, low = parts(through)
    real_left = jnp.concatenate([x[:, :HALO_PAD] for x in (high, low, high)], axis=1)
    imag_left = jnp.concatenate([x[:, HALO_PAD:] for x in (high, low, high)], axis=1)

    for at in range(2):
        copy_of(at).wait_recv()

    @pl.when(a < axial - 1)
    def _():
        for at in range(2, 5):
            copy_of(at).wait_recv()

    received_high, received_low = parts(halo_in[...] * halo_weights)
    right = jnp.concatenate([received_high, received_high, received_low], axis=0)
    real_cross = real_cross + dot(real_left, right)
    deliver(0, real_cross + real_cross.T)
    imag_cross = imag_cross + dot(imag_left, right)
    deliver(1, imag_cross - imag_cross.T)

    for at in range(2):
        copy_of(at).wait_send()

    @pl.when(a > 0)
    def _():
        for at in range(2, 5):
            copy_of(at).wait_send()


def plain_kernel(axial, circ, *refs):
    out_ref = refs[8]

    def deliver(part, value):
        out_ref[part] = value

    spectrum(axial, circ, refs[:8], refs[9:], [], deliver)


def coded(read, write, count):
    most = None
    for at in range(count):
        value = jnp.max(jnp.abs(read(at)), axis=0, keepdims=True)
        most = value if most is None else jnp.maximum(most, value)
    most = jnp.maximum(most, 1e-30)
    factor = LIMIT / most
    for at in range(count):
        write(at, jnp.round(read(at) * factor).astype(jnp.int32).astype(jnp.int16))
    return jnp.broadcast_to(most * (1.0 / LIMIT), (8, most.shape[1]))


def decoded(value, scales):
    return value.astype(jnp.int32).astype(jnp.float32) * scales[0:1]


def full_kernel(axial, circ, *refs):
    operands, out_ref, scratch = refs[:8], refs[8], refs[9:23]
    pieces, sent, came, sent_scale, came_scale, send_sem, recv_sem = refs[23:]
    a, c = lax.axis_index("axial"), lax.axis_index("circ")
    depth = axial // 4
    core, y, z = lax.rem(a, 2), lax.rem(a // 2, 2), a // 4
    flip_core = (a + 1 - 2 * core, c)
    first = (a + core * (2 - 4 * y), c + (1 - core) * (1 - 2 * c))
    second = (a + (1 - core) * (2 - 4 * y), c + core * (1 - 2 * c))
    key1 = core * y + (1 - core) * c
    key2 = core * c + (1 - core) * y
    slices = [(lax.rem(z + d, depth) * 4 + lax.rem(a, 4), c) for d in range(1, depth)]
    rows, columns = out_ref.shape[1:]
    base = (0, 4 * depth, 6 * depth) + tuple(7 * depth + d for d in range(depth - 1))
    copies = {}

    def send(part, step, read, count, device):
        def write(at, value):
            sent[part, base[step] + at] = value

        sent_scale[part, step] = coded(read, write, count)
        span = pl.ds(base[step], count)
        for at, (source, target) in enumerate(
            ((sent.at[part, span], came.at[part, span]), (sent_scale.at[part, step], came_scale.at[part, step]))
        ):
            copy = pltpu.make_async_remote_copy(
                src_ref=source,
                dst_ref=target,
                send_sem=send_sem.at[part, step, at],
                recv_sem=recv_sem.at[part, step, at],
                device_id=device,
                device_id_type=MESH,
            )
            copy.start()
            copies[part, step, at] = copy

    def receive(part, step):
        for at in range(2):
            copies[part, step, at].wait_recv()
        return came_scale[part, step]

    def deliver(part, value):
        for to_core in range(2):
            for to_y in range(2):
                for to_x in range(2):
                    for to_z in range(depth):
                        start = (to_z * 4 + to_y * 2 + to_core) * rows
                        place = (to_core,) + ((to_x, to_y) if to_core == 0 else (to_y, to_x))
                        at = ((place[0] * 2 + place[1]) * 2 + place[2]) * depth + to_z
                        pieces[part, at] = value[start : start + rows, to_x * columns : (to_x + 1) * columns]
        other = (1 - core) * 4 * depth
        send(part, 0, lambda at: pieces[part, other + at], 4 * depth, flip_core)

    spectrum(axial, circ, operands, scratch, [flip_core, first, second] + slices, deliver)

    def add(part, step, scales, own, offset, count):
        for at in range(count):
            pieces[part, own + offset + at] += decoded(came[part, base[step] + offset + at], scales)

    for part in range(2):
        scales = receive(part, 0)
        own, give, keep = core * 4 * depth, (1 - key1) * 2 * depth, key1 * 2 * depth
        add(part, 0, scales, own, give, 2 * depth)
        send(part, 1, lambda at: pieces[part, own + give + at], 2 * depth, first)
        add(part, 0, scales, own, keep, 2 * depth)
    for part in range(2):
        scales = receive(part, 1)
        own, give, keep = core * 4 * depth + key1 * 2 * depth, (1 - key2) * depth, key2 * depth
        add(part, 1, scales, own, give, depth)
        send(part, 2, lambda at: pieces[part, own + give + at], depth, second)
        add(part, 1, scales, own, keep, depth)
    for part in range(2):
        scales = receive(part, 2)
        own = core * 4 * depth + key1 * 2 * depth + key2 * depth
        add(part, 2, scales, own, 0, depth)
        for d in range(1, depth):
            send(part, 2 + d, lambda at: pieces[part, own + lax.rem(z + d, depth)], 1, slices[d - 1])
    for part in range(2):
        total = pieces[part, own + z]
        for d in range(1, depth):
            scales = receive(part, 2 + d)
            total = total + decoded(came[part, base[2 + d]], scales)
        out_ref[part] = total
    for copy in copies.values():
        copy.wait_send()


def solution(mesh):
    axial, circ = mesh.shape["axial"], mesh.shape["circ"]

    def body(mode_shapes, amplitude, pair_list, pair_counts):
        modes = mode_shapes.shape[-1]
        constants = tables()
        rows, columns = modes // axial, modes // circ
        vmem, hbm = pl.BlockSpec(memory_space=pltpu.VMEM), pl.BlockSpec(memory_space=pltpu.HBM)
        scratch = [
            pltpu.VMEM((HALO, modes), jnp.float32),
            pltpu.VMEM((HALO_PAD, modes), jnp.float32),
            pltpu.SemaphoreType.DMA((5,)),
            pltpu.SemaphoreType.DMA((5,)),
            pltpu.VMEM((4 * PATCH, modes), jnp.bfloat16),
            pltpu.VMEM(mode_shapes.shape, jnp.float32),
        ]
        scratch += [pltpu.VMEM(value.shape, jnp.bfloat16) for value in constants[:3]]
        listing = pair_list.reshape(3, 1, -1)
        scratch += [
            pltpu.VMEM(amplitude.shape, jnp.float32),
            pltpu.VMEM(listing.shape, jnp.int32),
            pltpu.VMEM((1, 1), jnp.int32),
            pltpu.VMEM((HALO_PAD, 1), jnp.int32),
            pltpu.SemaphoreType.DMA((11,)),
        ]
        together = circ == 2 and axial % 4 == 0 and rows % 32 == 0 and columns % 128 == 0
        depth = axial // 4
        if together:
            kernel, shape = full_kernel, (2, rows, columns)
            steps, total = 2 + depth, 8 * depth
            scratch += [
                pltpu.VMEM((2, 8 * depth, rows, columns), jnp.float32),
                pltpu.VMEM((2, total, rows, columns), jnp.int16),
                pltpu.VMEM((2, total, rows, columns), jnp.int16),
                pltpu.VMEM((2, steps, 8, columns), jnp.float32),
                pltpu.VMEM((2, steps, 8, columns), jnp.float32),
                pltpu.SemaphoreType.DMA((2, steps, 2)),
                pltpu.SemaphoreType.DMA((2, steps, 2)),
            ]
        else:
            kernel, shape = plain_kernel, (2, modes, modes)
        result = pl.pallas_call(
            functools.partial(kernel, axial, circ),
            out_shape=jax.ShapeDtypeStruct(shape, jnp.float32),
            in_specs=[hbm] * 8,
            out_specs=vmem,
            scratch_shapes=scratch,
            compiler_params=pltpu.CompilerParams(collective_id=0, has_side_effects=True, vmem_limit_bytes=56 * 1024 * 1024),
        )(mode_shapes, amplitude, listing, pair_counts, *constants)
        if not together:
            result = lax.psum_scatter(result, "axial", scatter_dimension=1, tiled=True)
            result = lax.psum_scatter(result, "circ", scatter_dimension=2, tiled=True)
        return result

    in_specs = (
        P("axial", "circ", None, None),
        P("axial", "circ", None),
        P("axial", "circ", None, None),
        P("axial", "circ"),
    )
    return jax.shard_map(body, mesh=mesh, in_specs=in_specs, out_specs=P(None, "axial", "circ"), check_vma=False)
```

```python
import functools

import numpy as np
import ml_dtypes
import jax
import jax.numpy as jnp
from jax import lax
from jax.experimental import pallas as pl
from jax.experimental.pallas import tpu as pltpu
from jax.sharding import PartitionSpec as P

ALONG = 16
AROUND = 8
PATCH = ALONG * AROUND
DECAY_A = 0.125
DECAY_C = 0.16
WAVE = 0.6
KINDS = ((0, 0), (0, 1), (1, -1), (1, 0), (1, 1))
HALO = 112
HALO_PAD = 128
LIMIT = 32767.0
MESH = pl.DeviceIdType.MESH


def split(values):
    high = values.astype(ml_dtypes.bfloat16)
    low = (values - high.astype(np.float64)).astype(ml_dtypes.bfloat16)
    return high, low


@functools.lru_cache(None)
def tables():
    index = np.arange(PATCH)
    along, around = index // AROUND, index % AROUND
    tiles = []
    for step_a, step_c in KINDS:
        gap_a = (step_a * ALONG + along[None, :] - along[:, None]).astype(np.float32)
        gap_c = (step_c * AROUND + around[None, :] - around[:, None]).astype(np.float32)
        weight = np.float32(0.5 if (step_a, step_c) == (0, 0) else 1.0)
        envelope = weight * np.exp(np.float32(-DECAY_A) * np.abs(gap_a) - np.float32(DECAY_C) * np.abs(gap_c))
        angle = np.float32(WAVE) * gap_a
        tiles.append(np.concatenate([envelope * np.cos(angle), -envelope * np.sin(angle)]))
    tiles = np.stack(tiles).astype(ml_dtypes.bfloat16)

    g = np.zeros((40, PATCH))
    forward = np.exp(-DECAY_C * around)
    backward = np.exp(-DECAY_C * (AROUND - around))
    phase = np.exp((-DECAY_A - 1j * WAVE) * along)
    for k in range(ALONG):
        g[k] = forward * (along == k)
    for k in range(AROUND):
        g[16 + k] = phase.real * (around == k)
        g[24 + k] = phase.imag * (around == k)
    g[32], g[33] = (phase * forward).real, (phase * forward).imag
    g[34], g[35] = (phase * backward).real, (phase * backward).imag
    gather = np.concatenate(split(g))

    spread = np.zeros((4, PATCH, HALO_PAD), np.complex128)
    code = np.full((HALO_PAD, 1), -1, np.int32)
    alpha = np.exp((-DECAY_A - 1j * WAVE) * (ALONG - along))
    ahead = np.exp(-DECAY_C * (AROUND - around))
    behind = np.exp(-DECAY_C * around)

    def around_sums(block, base):
        for k in range(ALONG):
            gap = k - along
            spread[block, :, base + k] = np.exp(-DECAY_A * np.abs(gap) - 1j * WAVE * gap) * ahead
            code[base + k] = block * 5 + 1

    def along_sums(block, base):
        for k in range(AROUND):
            value = alpha * np.exp(-DECAY_C * np.abs(k - around))
            spread[block, :, base + k] = value
            spread[block, :, base + 8 + k] = 1j * value
            code[base + k] = code[base + 8 + k] = block * 5 + 3

    def both_sums(block, base, kind):
        value = alpha * (ahead if kind == 4 else behind)
        spread[block, :, base] = value
        spread[block, :, base + 1] = 1j * value
        code[base] = code[base + 1] = block * 5 + kind

    around_sums(1, 0)
    around_sums(3, 16)
    both_sums(1, 32, 4)
    both_sums(0, 40 + 2, 2)
    along_sums(2, 48)
    both_sums(3, 48 + 18, 2)
    along_sums(3, 72)
    both_sums(2, 72 + 16, 4)
    both_sums(3, 96, 4)
    both_sums(2, 104 + 2, 2)
    spread = spread.reshape(4 * PATCH, HALO_PAD)
    spread = np.stack(split(np.concatenate([spread.real, spread.imag], axis=1)))
    return tiles, gather, spread, code


LOCAL = ((0, 1, 3, 4), (0, 2, 3), (0, 1), (0,))
MESSAGES = ((0, -1, 0, 40), (0, 1, 40, 8), (-1, 0, 48, 48), (-1, -1, 96, 8), (-1, 1, 104, 8))


def parts(value):
    high = value.astype(jnp.bfloat16)
    return high, (value - high.astype(jnp.float32)).astype(jnp.bfloat16)


def dot(a, b):
    return jnp.dot(a, b, preferred_element_type=jnp.float32)


def spectrum(axial, circ, operands, scratch, relations, deliver):
    shapes_hbm, amp_hbm, list_hbm, count_hbm, tiles_hbm, gather_hbm, spread_hbm, code_hbm = operands
    halo_out, halo_in, halo_send, halo_recv, weighted, shapes_ref, tiles_ref, gather_ref, spread_ref, amp_ref, list_ref, count_ref, code_ref, fetch_sem = scratch
    fetches = [
        pltpu.make_async_copy(source, target, fetch_sem.at[at])
        for at, (source, target) in enumerate(
            [(gather_hbm, gather_ref)]
            + [(shapes_hbm.at[block // 2, block % 2], shapes_ref.at[block // 2, block % 2]) for block in range(4)]
            + [(tiles_hbm, tiles_ref), (spread_hbm, spread_ref)]
            + [(amp_hbm, amp_ref), (list_hbm, list_ref), (count_hbm, count_ref), (code_hbm, code_ref)]
        )
    ]
    for fetch in fetches:
        fetch.start()
    a, c = lax.axis_index("axial"), lax.axis_index("circ")
    modes = weighted.shape[-1]

    def device(step_a, step_c):
        return (lax.rem(a + step_a + axial, axial), lax.rem(c + step_c + circ, circ))

    halo_in[...] = jnp.zeros_like(halo_in)
    barrier = pltpu.get_barrier_semaphore()
    steps = {(s * sa, s * sc % circ) for sa, sc, _, _ in MESSAGES for s in (1, -1)}
    greeted = [device(sa, sc) for sa, sc in sorted(steps)] + relations
    for target in greeted:
        pl.semaphore_signal(barrier, inc=1, device_id=target, device_id_type=MESH)

    sums = []
    fetches[0].wait()
    fetches[7].wait()
    for block in range(4):
        fetches[1 + block].wait()
        i, j = block // 2, block % 2
        column = jnp.broadcast_to(amp_ref[i, j : j + 1, :], (PATCH, PATCH)).T
        wide = jnp.concatenate([column] * (modes // PATCH), axis=1)
        weighted[block * PATCH : (block + 1) * PATCH, :] = (shapes_ref[i, j] * wide).astype(jnp.bfloat16)
        both = dot(gather_ref[...], weighted[block * PATCH : (block + 1) * PATCH, :])
        sums.append(both[:40] + both[40:])
    halo_out[0:16] = sums[0][0:16]
    halo_out[16:32] = sums[2][0:16]
    halo_out[32:40] = sums[2][32:40]
    halo_out[40:48] = sums[3][32:40]
    halo_out[48:72] = sums[0][16:40]
    halo_out[72:96] = sums[1][16:40]
    halo_out[96:104] = sums[0][32:40]
    halo_out[104:112] = sums[1][32:40]
    pl.semaphore_wait(barrier, len(greeted))

    def copy_of(at):
        step_a, step_c, base, rows = MESSAGES[at]
        return pltpu.make_async_remote_copy(
            src_ref=halo_out.at[pl.ds(base, rows)],
            dst_ref=halo_in.at[pl.ds(base, rows)],
            send_sem=halo_send.at[at],
            recv_sem=halo_recv.at[at],
            device_id=device(step_a, step_c),
            device_id_type=MESH,
        )

    for at in range(2):
        copy_of(at).start()

    @pl.when(a > 0)
    def _():
        for at in range(2, 5):
            copy_of(at).start()

    for at in range(8, 11):
        fetches[at].wait()
    slot_code = list_ref[0] * 5 + list_ref[1] * 3 + list_ref[2]
    kept = lax.broadcasted_iota(jnp.int32, slot_code.shape, 1) < count_ref[...]
    slot_code = jnp.where(kept, slot_code, -2)
    wanted = lax.broadcasted_iota(jnp.int32, (24, slot_code.shape[1]), 0)
    weights = jnp.sum(jnp.where(wanted == slot_code, 1.0, 0.0), axis=1, keepdims=True)
    halo_weights = jnp.sum(jnp.where(code_ref[...] == slot_code, 1.0, 0.0), axis=1, keepdims=True)

    fetches[5].wait()
    real_sums, imag_sums = [], []
    for block in range(4):
        tiles = []
        for kind in LOCAL[block]:
            at = block * 5 + kind
            tiles.append(tiles_ref[kind] * jnp.broadcast_to(weights[at : at + 1], (2 * PATCH, PATCH)).astype(jnp.bfloat16))
        tile = tiles[0] if len(tiles) == 1 else jnp.concatenate(tiles, axis=1)
        total = dot(tile, weighted[(4 - len(tiles)) * PATCH :, :])
        real_sums.append(total[:PATCH])
        imag_sums.append(total[PATCH:])
    turned = weighted[...].T
    real_high, real_low = parts(jnp.concatenate(real_sums, axis=0))
    imag_high, imag_low = parts(jnp.concatenate(imag_sums, axis=0))
    real_cross = dot(turned, real_high) + dot(turned, real_low)
    imag_cross = dot(turned, imag_high) + dot(turned, imag_low)
    fetches[6].wait()
    through = dot(turned, spread_ref[0]) + dot(turned, spread_ref[1])
    high, low = parts(through)
    real_left = jnp.concatenate([x[:, :HALO_PAD] for x in (high, low, high)], axis=1)
    imag_left = jnp.concatenate([x[:, HALO_PAD:] for x in (high, low, high)], axis=1)

    for at in range(2):
        copy_of(at).wait_recv()

    @pl.when(a < axial - 1)
    def _():
        for at in range(2, 5):
            copy_of(at).wait_recv()

    received_high, received_low = parts(halo_in[...] * halo_weights)
    right = jnp.concatenate([received_high, received_high, received_low], axis=0)
    real_cross = real_cross + dot(real_left, right)
    deliver(0, real_cross + real_cross.T)
    imag_cross = imag_cross + dot(imag_left, right)
    deliver(1, imag_cross - imag_cross.T)

    for at in range(2):
        copy_of(at).wait_send()

    @pl.when(a > 0)
    def _():
        for at in range(2, 5):
            copy_of(at).wait_send()


def plain_kernel(axial, circ, *refs):
    out_ref = refs[8]

    def deliver(part, value):
        out_ref[part] = value

    spectrum(axial, circ, refs[:8], refs[9:], [], deliver)


def coded(read, write, count):
    most = None
    for at in range(count):
        value = jnp.max(jnp.abs(read(at)), axis=0, keepdims=True)
        most = value if most is None else jnp.maximum(most, value)
    most = jnp.maximum(most, 1e-30)
    factor = LIMIT / most
    for at in range(count):
        write(at, jnp.round(read(at) * factor).astype(jnp.int32).astype(jnp.int16))
    return most * (1.0 / LIMIT)


def decoded(value, scales):
    return value.astype(jnp.int32).astype(jnp.float32) * scales


def full_kernel(axial, circ, *refs):
    operands, out_ref, scratch = refs[:8], refs[8], refs[9:23]
    pieces, sent, came, sent_scale, came_scale, send_sem, recv_sem = refs[23:]
    a, c = lax.axis_index("axial"), lax.axis_index("circ")
    depth = axial // 4
    core, y, z = lax.rem(a, 2), lax.rem(a // 2, 2), a // 4
    flip_core = (a + 1 - 2 * core, c)
    first = (a + core * (2 - 4 * y), c + (1 - core) * (1 - 2 * c))
    second = (a + (1 - core) * (2 - 4 * y), c + core * (1 - 2 * c))
    key1 = core * y + (1 - core) * c
    key2 = core * c + (1 - core) * y
    slices = [(lax.rem(z + d, depth) * 4 + lax.rem(a, 4), c) for d in range(1, depth)]
    rows, columns = out_ref.shape[1:]
    base = (0, 4 * depth, 6 * depth) + tuple(7 * depth + d for d in range(depth - 1))
    copies = {}

    def send(part, step, read, count, device):
        def write(at, value):
            sent[part, base[step] + at] = value

        sent_scale[part, step] = coded(read, write, count)
        span = pl.ds(base[step], count)
        for at, (source, target) in enumerate(
            ((sent.at[part, span], came.at[part, span]), (sent_scale.at[part, step], came_scale.at[part, step]))
        ):
            copy = pltpu.make_async_remote_copy(
                src_ref=source,
                dst_ref=target,
                send_sem=send_sem.at[part, step, at],
                recv_sem=recv_sem.at[part, step, at],
                device_id=device,
                device_id_type=MESH,
            )
            copy.start()
            copies[part, step, at] = copy

    def receive(part, step):
        for at in range(2):
            copies[part, step, at].wait_recv()
        return came_scale[part, step]

    def deliver(part, value):
        for to_core in range(2):
            for to_y in range(2):
                for to_x in range(2):
                    for to_z in range(depth):
                        start = (to_z * 4 + to_y * 2 + to_core) * rows
                        place = (to_core,) + ((to_x, to_y) if to_core == 0 else (to_y, to_x))
                        at = ((place[0] * 2 + place[1]) * 2 + place[2]) * depth + to_z
                        pieces[part, at] = value[start : start + rows, to_x * columns : (to_x + 1) * columns]
        other = (1 - core) * 4 * depth
        send(part, 0, lambda at: pieces[part, other + at], 4 * depth, flip_core)

    spectrum(axial, circ, operands, scratch, [flip_core, first, second] + slices, deliver)

    def add(part, step, scales, own, offset, count):
        for at in range(count):
            pieces[part, own + offset + at] += decoded(came[part, base[step] + offset + at], scales)

    for part in range(2):
        scales = receive(part, 0)
        own, give, keep = core * 4 * depth, (1 - key1) * 2 * depth, key1 * 2 * depth
        add(part, 0, scales, own, give, 2 * depth)
        send(part, 1, lambda at: pieces[part, own + give + at], 2 * depth, first)
    for part in range(2):
        add(part, 0, came_scale[part, 0], own, keep, 2 * depth)
    for part in range(2):
        scales = receive(part, 1)
        own, give, keep = core * 4 * depth + key1 * 2 * depth, (1 - key2) * depth, key2 * depth
        add(part, 1, scales, own, give, depth)
        send(part, 2, lambda at: pieces[part, own + give + at], depth, second)
    for part in range(2):
        add(part, 1, came_scale[part, 1], own, keep, depth)
    for part in range(2):
        scales = receive(part, 2)
        own = core * 4 * depth + key1 * 2 * depth + key2 * depth
        add(part, 2, scales, own, 0, depth)
        for d in range(1, depth):
            send(part, 2 + d, lambda at: pieces[part, own + lax.rem(z + d, depth)], 1, slices[d - 1])
    for part in range(2):
        total = pieces[part, own + z]
        for d in range(1, depth):
            scales = receive(part, 2 + d)
            total = total + decoded(came[part, base[2 + d]], scales)
        out_ref[part] = total
    for copy in copies.values():
        copy.wait_send()


def solution(mesh):
    axial, circ = mesh.shape["axial"], mesh.shape["circ"]

    def body(mode_shapes, amplitude, pair_list, pair_counts):
        modes = mode_shapes.shape[-1]
        constants = tables()
        rows, columns = modes // axial, modes // circ
        vmem, hbm = pl.BlockSpec(memory_space=pltpu.VMEM), pl.BlockSpec(memory_space=pltpu.HBM)
        scratch = [
            pltpu.VMEM((HALO, modes), jnp.float32),
            pltpu.VMEM((HALO_PAD, modes), jnp.float32),
            pltpu.SemaphoreType.DMA((5,)),
            pltpu.SemaphoreType.DMA((5,)),
            pltpu.VMEM((4 * PATCH, modes), jnp.bfloat16),
            pltpu.VMEM(mode_shapes.shape, jnp.float32),
        ]
        scratch += [pltpu.VMEM(value.shape, jnp.bfloat16) for value in constants[:3]]
        listing = pair_list.reshape(3, 1, -1)
        scratch += [
            pltpu.VMEM(amplitude.shape, jnp.float32),
            pltpu.VMEM(listing.shape, jnp.int32),
            pltpu.VMEM((1, 1), jnp.int32),
            pltpu.VMEM((HALO_PAD, 1), jnp.int32),
            pltpu.SemaphoreType.DMA((11,)),
        ]
        together = circ == 2 and axial % 4 == 0 and rows % 32 == 0 and columns % 128 == 0
        depth = axial // 4
        if together:
            kernel, shape = full_kernel, (2, rows, columns)
            steps, total = 2 + depth, 8 * depth
            scratch += [
                pltpu.VMEM((2, 8 * depth, rows, columns), jnp.float32),
                pltpu.VMEM((2, total, rows, columns), jnp.int16),
                pltpu.VMEM((2, total, rows, columns), jnp.int16),
                pltpu.VMEM((2, steps, 1, columns), jnp.float32),
                pltpu.VMEM((2, steps, 1, columns), jnp.float32),
                pltpu.SemaphoreType.DMA((2, steps, 2)),
                pltpu.SemaphoreType.DMA((2, steps, 2)),
            ]
        else:
            kernel, shape = plain_kernel, (2, modes, modes)
        result = pl.pallas_call(
            functools.partial(kernel, axial, circ),
            out_shape=jax.ShapeDtypeStruct(shape, jnp.float32),
            in_specs=[hbm] * 8,
            out_specs=vmem,
            scratch_shapes=scratch,
            compiler_params=pltpu.CompilerParams(collective_id=0, has_side_effects=True, vmem_limit_bytes=56 * 1024 * 1024),
        )(mode_shapes, amplitude, listing, pair_counts, *constants)
        if not together:
            result = lax.psum_scatter(result, "axial", scatter_dimension=1, tiled=True)
            result = lax.psum_scatter(result, "circ", scatter_dimension=2, tiled=True)
        return result

    in_specs = (
        P("axial", "circ", None, None),
        P("axial", "circ", None),
        P("axial", "circ", None, None),
        P("axial", "circ"),
    )
    return jax.shard_map(body, mesh=mesh, in_specs=in_specs, out_specs=P(None, "axial", "circ"), check_vma=False)
```

```python
import functools

import numpy as np
import ml_dtypes
import jax
import jax.numpy as jnp
from jax import lax
from jax.experimental import pallas as pl
from jax.experimental.pallas import tpu as pltpu
from jax.sharding import PartitionSpec as P

ALONG = 16
AROUND = 8
PATCH = ALONG * AROUND
DECAY_A = 0.125
DECAY_C = 0.16
WAVE = 0.6
KINDS = ((0, 0), (0, 1), (1, -1), (1, 0), (1, 1))
HALO = 112
HALO_PAD = 128
LIMIT = 32767.0
MESH = pl.DeviceIdType.MESH


def split(values):
    high = values.astype(ml_dtypes.bfloat16)
    low = (values - high.astype(np.float64)).astype(ml_dtypes.bfloat16)
    return high, low


@functools.lru_cache(None)
def tables():
    index = np.arange(PATCH)
    along, around = index // AROUND, index % AROUND
    tiles = []
    for step_a, step_c in KINDS:
        gap_a = (step_a * ALONG + along[None, :] - along[:, None]).astype(np.float32)
        gap_c = (step_c * AROUND + around[None, :] - around[:, None]).astype(np.float32)
        weight = np.float32(0.5 if (step_a, step_c) == (0, 0) else 1.0)
        envelope = weight * np.exp(np.float32(-DECAY_A) * np.abs(gap_a) - np.float32(DECAY_C) * np.abs(gap_c))
        angle = np.float32(WAVE) * gap_a
        tiles.append(np.concatenate([envelope * np.cos(angle), -envelope * np.sin(angle)]))
    tiles = np.stack(tiles).astype(ml_dtypes.bfloat16)

    g = np.zeros((40, PATCH))
    forward = np.exp(-DECAY_C * around)
    backward = np.exp(-DECAY_C * (AROUND - around))
    phase = np.exp((-DECAY_A - 1j * WAVE) * along)
    for k in range(ALONG):
        g[k] = forward * (along == k)
    for k in range(AROUND):
        g[16 + k] = phase.real * (around == k)
        g[24 + k] = phase.imag * (around == k)
    g[32], g[33] = (phase * forward).real, (phase * forward).imag
    g[34], g[35] = (phase * backward).real, (phase * backward).imag
    gather = np.concatenate(split(g))

    spread = np.zeros((4, PATCH, HALO_PAD), np.complex128)
    code = np.full((HALO_PAD, 1), -1, np.int32)
    alpha = np.exp((-DECAY_A - 1j * WAVE) * (ALONG - along))
    ahead = np.exp(-DECAY_C * (AROUND - around))
    behind = np.exp(-DECAY_C * around)

    def around_sums(block, base):
        for k in range(ALONG):
            gap = k - along
            spread[block, :, base + k] = np.exp(-DECAY_A * np.abs(gap) - 1j * WAVE * gap) * ahead
            code[base + k] = block * 5 + 1

    def along_sums(block, base):
        for k in range(AROUND):
            value = alpha * np.exp(-DECAY_C * np.abs(k - around))
            spread[block, :, base + k] = value
            spread[block, :, base + 8 + k] = 1j * value
            code[base + k] = code[base + 8 + k] = block * 5 + 3

    def both_sums(block, base, kind):
        value = alpha * (ahead if kind == 4 else behind)
        spread[block, :, base] = value
        spread[block, :, base + 1] = 1j * value
        code[base] = code[base + 1] = block * 5 + kind

    around_sums(1, 0)
    around_sums(3, 16)
    both_sums(1, 32, 4)
    both_sums(0, 40 + 2, 2)
    along_sums(2, 48)
    both_sums(3, 48 + 18, 2)
    along_sums(3, 72)
    both_sums(2, 72 + 16, 4)
    both_sums(3, 96, 4)
    both_sums(2, 104 + 2, 2)
    spread = spread.reshape(4 * PATCH, HALO_PAD)
    spread = np.stack(split(np.concatenate([spread.real, spread.imag], axis=1)))
    return tiles, gather, spread, code


LOCAL = ((0, 1, 3, 4), (0, 2, 3), (0, 1), (0,))
MESSAGES = ((0, -1, 0, 40), (0, 1, 40, 8), (-1, 0, 48, 48), (-1, -1, 96, 8), (-1, 1, 104, 8))


def parts(value):
    high = value.astype(jnp.bfloat16)
    return high, (value - high.astype(jnp.float32)).astype(jnp.bfloat16)


def dot(a, b):
    return jnp.dot(a, b, preferred_element_type=jnp.float32)


def spectrum(axial, circ, operands, scratch, relations, deliver):
    shapes_hbm, amp_hbm, list_hbm, count_hbm, tiles_hbm, gather_hbm, spread_hbm, code_hbm = operands
    halo_out, halo_in, halo_send, halo_recv, weighted, shapes_ref, tiles_ref, gather_ref, spread_ref, amp_ref, list_ref, count_ref, code_ref, fetch_sem = scratch
    fetches = [
        pltpu.make_async_copy(source, target, fetch_sem.at[at])
        for at, (source, target) in enumerate(
            [(gather_hbm, gather_ref)]
            + [(shapes_hbm.at[block // 2, block % 2], shapes_ref.at[block // 2, block % 2]) for block in range(4)]
            + [(tiles_hbm, tiles_ref), (spread_hbm, spread_ref)]
            + [(amp_hbm, amp_ref), (list_hbm, list_ref), (count_hbm, count_ref), (code_hbm, code_ref)]
        )
    ]
    for fetch in fetches[7:] + fetches[:7]:
        fetch.start()
    a, c = lax.axis_index("axial"), lax.axis_index("circ")
    modes = weighted.shape[-1]

    def device(step_a, step_c):
        return (lax.rem(a + step_a + axial, axial), lax.rem(c + step_c + circ, circ))

    halo_in[...] = jnp.zeros_like(halo_in)
    barrier = pltpu.get_barrier_semaphore()
    steps = {(s * sa, s * sc % circ) for sa, sc, _, _ in MESSAGES for s in (1, -1)}
    greeted = [device(sa, sc) for sa, sc in sorted(steps)] + relations
    for target in greeted:
        pl.semaphore_signal(barrier, inc=1, device_id=target, device_id_type=MESH)

    sums = []
    fetches[0].wait()
    fetches[7].wait()
    for block in range(4):
        fetches[1 + block].wait()
        i, j = block // 2, block % 2
        column = jnp.broadcast_to(amp_ref[i, j : j + 1, :], (PATCH, PATCH)).T
        wide = jnp.concatenate([column] * (modes // PATCH), axis=1)
        weighted[block * PATCH : (block + 1) * PATCH, :] = (shapes_ref[i, j] * wide).astype(jnp.bfloat16)
        both = dot(gather_ref[...], weighted[block * PATCH : (block + 1) * PATCH, :])
        sums.append(both[:40] + both[40:])
    halo_out[0:16] = sums[0][0:16]
    halo_out[16:32] = sums[2][0:16]
    halo_out[32:40] = sums[2][32:40]
    halo_out[40:48] = sums[3][32:40]
    halo_out[48:72] = sums[0][16:40]
    halo_out[72:96] = sums[1][16:40]
    halo_out[96:104] = sums[0][32:40]
    halo_out[104:112] = sums[1][32:40]
    pl.semaphore_wait(barrier, len(greeted))

    def copy_of(at):
        step_a, step_c, base, rows = MESSAGES[at]
        return pltpu.make_async_remote_copy(
            src_ref=halo_out.at[pl.ds(base, rows)],
            dst_ref=halo_in.at[pl.ds(base, rows)],
            send_sem=halo_send.at[at],
            recv_sem=halo_recv.at[at],
            device_id=device(step_a, step_c),
            device_id_type=MESH,
        )

    for at in range(2):
        copy_of(at).start()

    @pl.when(a > 0)
    def _():
        for at in range(2, 5):
            copy_of(at).start()

    for at in range(8, 11):
        fetches[at].wait()
    slot_code = list_ref[0] * 5 + list_ref[1] * 3 + list_ref[2]
    kept = lax.broadcasted_iota(jnp.int32, slot_code.shape, 1) < count_ref[...]
    slot_code = jnp.where(kept, slot_code, -2)
    wanted = lax.broadcasted_iota(jnp.int32, (24, slot_code.shape[1]), 0)
    weights = jnp.sum(jnp.where(wanted == slot_code, 1.0, 0.0), axis=1, keepdims=True)
    halo_weights = jnp.sum(jnp.where(code_ref[...] == slot_code, 1.0, 0.0), axis=1, keepdims=True)

    fetches[5].wait()
    real_sums, imag_sums = [], []
    for block in range(4):
        tiles = []
        for kind in LOCAL[block]:
            at = block * 5 + kind
            tiles.append(tiles_ref[kind] * jnp.broadcast_to(weights[at : at + 1], (2 * PATCH, PATCH)).astype(jnp.bfloat16))
        tile = tiles[0] if len(tiles) == 1 else jnp.concatenate(tiles, axis=1)
        total = dot(tile, weighted[(4 - len(tiles)) * PATCH :, :])
        real_sums.append(total[:PATCH])
        imag_sums.append(total[PATCH:])
    turned = weighted[...].T
    real_high, real_low = parts(jnp.concatenate(real_sums, axis=0))
    imag_high, imag_low = parts(jnp.concatenate(imag_sums, axis=0))
    real_cross = dot(turned, real_high) + dot(turned, real_low)
    imag_cross = dot(turned, imag_high) + dot(turned, imag_low)
    fetches[6].wait()
    through = dot(turned, spread_ref[0]) + dot(turned, spread_ref[1])
    high, low = parts(through)
    real_left = jnp.concatenate([x[:, :HALO_PAD] for x in (high, low, high)], axis=1)
    imag_left = jnp.concatenate([x[:, HALO_PAD:] for x in (high, low, high)], axis=1)

    for at in range(2):
        copy_of(at).wait_recv()

    @pl.when(a < axial - 1)
    def _():
        for at in range(2, 5):
            copy_of(at).wait_recv()

    received_high, received_low = parts(halo_in[...] * halo_weights)
    right = jnp.concatenate([received_high, received_high, received_low], axis=0)
    real_cross = real_cross + dot(real_left, right)
    deliver(0, real_cross + real_cross.T)
    imag_cross = imag_cross + dot(imag_left, right)
    deliver(1, imag_cross - imag_cross.T)

    for at in range(2):
        copy_of(at).wait_send()

    @pl.when(a > 0)
    def _():
        for at in range(2, 5):
            copy_of(at).wait_send()


def plain_kernel(axial, circ, *refs):
    out_ref = refs[8]

    def deliver(part, value):
        out_ref[part] = value

    spectrum(axial, circ, refs[:8], refs[9:], [], deliver)


def coded(read, write, count):
    most = None
    for at in range(count):
        value = jnp.max(jnp.abs(read(at)), axis=0, keepdims=True)
        most = value if most is None else jnp.maximum(most, value)
    most = jnp.maximum(most, 1e-30)
    factor = LIMIT / most
    for at in range(count):
        write(at, jnp.round(read(at) * factor).astype(jnp.int32).astype(jnp.int16))
    return most * (1.0 / LIMIT)


def decoded(value, scales):
    return value.astype(jnp.int32).astype(jnp.float32) * scales


def full_kernel(axial, circ, *refs):
    operands, out_ref, scratch = refs[:8], refs[8], refs[9:23]
    pieces, sent, came, sent_scale, came_scale, send_sem, recv_sem = refs[23:]
    a, c = lax.axis_index("axial"), lax.axis_index("circ")
    depth = axial // 4
    core, y, z = lax.rem(a, 2), lax.rem(a // 2, 2), a // 4
    flip_core = (a + 1 - 2 * core, c)
    first = (a + core * (2 - 4 * y), c + (1 - core) * (1 - 2 * c))
    second = (a + (1 - core) * (2 - 4 * y), c + core * (1 - 2 * c))
    key1 = core * y + (1 - core) * c
    key2 = core * c + (1 - core) * y
    slices = [(lax.rem(z + d, depth) * 4 + lax.rem(a, 4), c) for d in range(1, depth)]
    rows, columns = out_ref.shape[1:]
    base = (0, 4 * depth, 6 * depth) + tuple(7 * depth + d for d in range(depth - 1))
    copies = {}

    def send(part, step, read, count, device):
        def write(at, value):
            sent[part, base[step] + at] = value

        sent_scale[part, step] = coded(read, write, count)
        span = pl.ds(base[step], count)
        for at, (source, target) in enumerate(
            ((sent.at[part, span], came.at[part, span]), (sent_scale.at[part, step], came_scale.at[part, step]))
        ):
            copy = pltpu.make_async_remote_copy(
                src_ref=source,
                dst_ref=target,
                send_sem=send_sem.at[part, step, at],
                recv_sem=recv_sem.at[part, step, at],
                device_id=device,
                device_id_type=MESH,
            )
            copy.start()
            copies[part, step, at] = copy

    def receive(part, step):
        for at in range(2):
            copies[part, step, at].wait_recv()
        return came_scale[part, step]

    def deliver(part, value):
        for to_core in range(2):
            for to_y in range(2):
                for to_x in range(2):
                    for to_z in range(depth):
                        start = (to_z * 4 + to_y * 2 + to_core) * rows
                        place = (to_core,) + ((to_x, to_y) if to_core == 0 else (to_y, to_x))
                        at = ((place[0] * 2 + place[1]) * 2 + place[2]) * depth + to_z
                        pieces[part, at] = value[start : start + rows, to_x * columns : (to_x + 1) * columns]
        other = (1 - core) * 4 * depth
        send(part, 0, lambda at: pieces[part, other + at], 4 * depth, flip_core)

    spectrum(axial, circ, operands, scratch, [flip_core, first, second] + slices, deliver)

    def add(part, step, scales, own, offset, count):
        for at in range(count):
            pieces[part, own + offset + at] += decoded(came[part, base[step] + offset + at], scales)

    for part in range(2):
        scales = receive(part, 0)
        own, give, keep = core * 4 * depth, (1 - key1) * 2 * depth, key1 * 2 * depth
        add(part, 0, scales, own, give, 2 * depth)
        send(part, 1, lambda at: pieces[part, own + give + at], 2 * depth, first)
    for part in range(2):
        add(part, 0, came_scale[part, 0], own, keep, 2 * depth)
    for part in range(2):
        scales = receive(part, 1)
        own, give, keep = core * 4 * depth + key1 * 2 * depth, (1 - key2) * depth, key2 * depth
        add(part, 1, scales, own, give, depth)
        send(part, 2, lambda at: pieces[part, own + give + at], depth, second)
    for part in range(2):
        add(part, 1, came_scale[part, 1], own, keep, depth)
    for part in range(2):
        scales = receive(part, 2)
        own = core * 4 * depth + key1 * 2 * depth + key2 * depth
        add(part, 2, scales, own, 0, depth)
        for d in range(1, depth):
            send(part, 2 + d, lambda at: pieces[part, own + lax.rem(z + d, depth)], 1, slices[d - 1])
    for part in range(2):
        total = pieces[part, own + z]
        for d in range(1, depth):
            scales = receive(part, 2 + d)
            total = total + decoded(came[part, base[2 + d]], scales)
        out_ref[part] = total
    for copy in copies.values():
        copy.wait_send()


def solution(mesh):
    axial, circ = mesh.shape["axial"], mesh.shape["circ"]

    def body(mode_shapes, amplitude, pair_list, pair_counts):
        modes = mode_shapes.shape[-1]
        constants = tables()
        rows, columns = modes // axial, modes // circ
        vmem, hbm = pl.BlockSpec(memory_space=pltpu.VMEM), pl.BlockSpec(memory_space=pltpu.HBM)
        scratch = [
            pltpu.VMEM((HALO, modes), jnp.float32),
            pltpu.VMEM((HALO_PAD, modes), jnp.float32),
            pltpu.SemaphoreType.DMA((5,)),
            pltpu.SemaphoreType.DMA((5,)),
            pltpu.VMEM((4 * PATCH, modes), jnp.bfloat16),
            pltpu.VMEM(mode_shapes.shape, jnp.float32),
        ]
        scratch += [pltpu.VMEM(value.shape, jnp.bfloat16) for value in constants[:3]]
        listing = pair_list.reshape(3, 1, -1)
        scratch += [
            pltpu.VMEM(amplitude.shape, jnp.float32),
            pltpu.VMEM(listing.shape, jnp.int32),
            pltpu.VMEM((1, 1), jnp.int32),
            pltpu.VMEM((HALO_PAD, 1), jnp.int32),
            pltpu.SemaphoreType.DMA((11,)),
        ]
        together = circ == 2 and axial % 4 == 0 and rows % 32 == 0 and columns % 128 == 0
        depth = axial // 4
        if together:
            kernel, shape = full_kernel, (2, rows, columns)
            steps, total = 2 + depth, 8 * depth
            scratch += [
                pltpu.VMEM((2, 8 * depth, rows, columns), jnp.float32),
                pltpu.VMEM((2, total, rows, columns), jnp.int16),
                pltpu.VMEM((2, total, rows, columns), jnp.int16),
                pltpu.VMEM((2, steps, 1, columns), jnp.float32),
                pltpu.VMEM((2, steps, 1, columns), jnp.float32),
                pltpu.SemaphoreType.DMA((2, steps, 2)),
                pltpu.SemaphoreType.DMA((2, steps, 2)),
            ]
        else:
            kernel, shape = plain_kernel, (2, modes, modes)
        result = pl.pallas_call(
            functools.partial(kernel, axial, circ),
            out_shape=jax.ShapeDtypeStruct(shape, jnp.float32),
            in_specs=[hbm] * 8,
            out_specs=vmem,
            scratch_shapes=scratch,
            compiler_params=pltpu.CompilerParams(collective_id=0, has_side_effects=True, vmem_limit_bytes=56 * 1024 * 1024),
        )(mode_shapes, amplitude, listing, pair_counts, *constants)
        if not together:
            result = lax.psum_scatter(result, "axial", scatter_dimension=1, tiled=True)
            result = lax.psum_scatter(result, "circ", scatter_dimension=2, tiled=True)
        return result

    in_specs = (
        P("axial", "circ", None, None),
        P("axial", "circ", None),
        P("axial", "circ", None, None),
        P("axial", "circ"),
    )
    return jax.shard_map(body, mesh=mesh, in_specs=in_specs, out_specs=P(None, "axial", "circ"), check_vma=False)
```
